128 devices in a mesh: row: 32 (over x, z_hi, y), col: 4 (over z_lo, core).
Axes of the slice: x: 4, y: 4, z: 4 (z_hi: 2, z_lo: 2; z = z_hi * 2 + z_lo), core: 2. Of those that a mesh axis runs over, the one named last changes fastest.
Arguments:
- pair_act: bfloat16 [768, 4096, 128], P('row', 'col'), may hold values from -6 to 6
- pair_cot: bfloat16 [768, 4096, 128], P('row', 'col'), may hold values from -6 to 6
- pair_mask: int32 [768, 4096], P('row', 'col'), may hold values 0 or 1
- pair_norm_gain: float32 [128], replicated, may hold values from 0.25 to 1.75
- pair_norm_bias: float32 [128], replicated, may hold values from -3 to 3
- proj_weight: bfloat16 [128, 128], replicated, may hold values from -0.5 to 0.5
- left_weight: bfloat16 [384, 128], replicated, may hold values from -0.3125 to 0.3125
- right_weight: bfloat16 [384, 128], replicated, may hold values from -0.3125 to 0.3125
Outputs:
- pair_activation_gradient: bfloat16 [768, 4096, 128], P('row', 'col')
- row_single_grad: float32 [768, 384], P('row')
- col_single_grad: float32 [4096, 384], P(('col', 'row'))
- weight_grad: float32 [128, 128], replicated
- gain_grad: float32 [128], replicated
- bias_grad: float32 [128], replicated
The draws below stay inside these ranges and needn't reach their ends.
All inputs are finite; a program needn't handle non-finite values. No bound on the sum of `pair_mask` on one device may be relied on, other than what follows from the above.
Results may differ from the reference program's by a relative error of at most 0.0031.
Values sent between devices are 32-bit elements; how exact they have to be, the bound alone decides.
No kernel may reach another device: no remote copies, remote signals or barrier semaphores. Data moves between devices by JAX's collectives and lax.ppermute only.
A program may use at most 128 MiB of HBM per device.

```python
import jax
import jax.numpy as jnp
from jax import lax

C = 128
S = 384
ROWS = 768
N = 4096


def plant(result, key, smallest, top_value):
    spot = [jax.random.randint(jax.random.fold_in(key, axis), (), 0, length) for axis, length in enumerate(result.shape)]
    main_axis = result.shape.index(max(result.shape))
    beside = spot[:main_axis] + [(spot[main_axis] + 1) % result.shape[main_axis]] + spot[main_axis + 1:]
    return result.at[tuple(spot)].set(smallest).at[tuple(beside)].set(top_value)


def with_spikes(values, rng, source, target, blocks, factor):
    def block_of(axis_at):
        return (jnp.arange(values.shape[axis_at]) // (values.shape[axis_at] // blocks)).reshape((-1,) + (1,) * (values.ndim - 1 - axis_at))

    first = jax.random.permutation(rng, blocks)[block_of(target)]
    second = (block_of(target) + blocks // 2) % blocks
    return jnp.where((block_of(source) == first) | (block_of(source) == second), factor * values, values)


def block_levels(stream_key, extent, split, least, largest):
    gain = 1.0
    for axis_at, parts in split:
        draws = jax.random.uniform(jax.random.fold_in(jax.random.fold_in(stream_key, 6), axis_at), (parts,), jnp.float32, least / len(split), largest / len(split))
        gain = gain * jnp.repeat(jnp.exp(draws), extent[axis_at] // parts).reshape((-1,) + (1,) * (len(extent) - 1 - axis_at))
    return gain


def normal_values(rng, dims, deviation, limit, cuts=(), held_as=jnp.bfloat16):
    array = deviation * jax.random.normal(rng, dims, jnp.float32)
    if cuts:
        array = array * block_levels(rng, dims, cuts, -0.22, 0.18)
    return jnp.clip(array, -limit, limit).astype(held_as)


def heavy_noise(key, shape, scale, reach, cuts, heavy, held_as=jnp.bfloat16):
    entries = scale * jax.random.normal(key, shape, jnp.float32)
    if cuts:
        entries = entries * block_levels(key, shape, cuts, -0.22, 0.18)
    return jnp.clip(with_spikes(entries, jax.random.fold_in(key, 3), *heavy), -reach, reach).astype(held_as)


def setup_inputs(seed: int = 0) -> dict:
    seeds = jax.random.split(jax.random.key(seed), 9)
    pair_act = normal_values(seeds[0], (ROWS, N, C), 1.0, 6.0, ((0, 32), (1, 4)))
    pair_cot = heavy_noise(seeds[1], (ROWS, N, C), 1.0, 6.0, ((0, 32), (1, 4)), (0, 1, 32, 2.75))
    pair_mask = plant((jax.random.randint(seeds[2], (ROWS, N), 0, 4) < 3).astype(jnp.int32), jax.random.fold_in(seeds[2], 1), 0, 1)
    pair_norm_gain = jnp.clip(1.0 + 0.15 * jax.random.normal(seeds[3], (C,), jnp.float32), 0.25, 1.75)
    pair_norm_bias = normal_values(seeds[4], (C,), 0.5, 3.0, (), jnp.float32)
    proj_weight = normal_values(seeds[5], (C, C), C ** -0.5, 0.5)
    left_weight = normal_values(seeds[6], (S, C), S ** -0.5, 0.3125)
    right_weight = normal_values(seeds[7], (S, C), S ** -0.5, 0.3125)
    return dict(pair_act=pair_act, pair_cot=pair_cot, pair_mask=pair_mask, pair_norm_gain=pair_norm_gain, pair_norm_bias=pair_norm_bias, proj_weight=proj_weight, left_weight=left_weight, right_weight=right_weight)


def block_terms(act, cot, mask, pair_norm_gain, pair_norm_bias, proj_weight):
    pair_input = act.astype(jnp.float32)
    pair_mean = lax.optimization_barrier(jnp.mean(pair_input, axis=-1, keepdims=True))
    var = lax.optimization_barrier(jnp.mean((pair_input - pair_mean) * (pair_input - pair_mean), axis=-1, keepdims=True))
    inverse_deviation = lax.rsqrt(var + 1e-05)
    standardized_input = (pair_input - pair_mean) * inverse_deviation
    normalized_pair = (standardized_input * pair_norm_gain + pair_norm_bias).astype(jnp.bfloat16)
    dz = cot * mask.astype(jnp.bfloat16)[..., None]
    normalized_gradient = jnp.einsum('rnd,ed->rne', dz.astype(jnp.float32), proj_weight.astype(jnp.float32))
    centered_gradient = normalized_gradient * pair_norm_gain
    first_term = lax.optimization_barrier(jnp.mean(centered_gradient, axis=-1, keepdims=True))
    second_term = lax.optimization_barrier(jnp.mean(centered_gradient * standardized_input, axis=-1, keepdims=True))
    pair_activation_gradient = (inverse_deviation * (centered_gradient - first_term - standardized_input * second_term)).astype(jnp.bfloat16)
    dzf = dz.astype(jnp.float32)
    weight_part = jnp.einsum('rnc,rnd->cd', normalized_pair.astype(jnp.float32), dzf)
    gain_partial = lax.optimization_barrier(jnp.sum(normalized_gradient * standardized_input, axis=(0, 1)))
    bias_part = lax.optimization_barrier(jnp.sum(normalized_gradient, axis=(0, 1)))
    return (pair_activation_gradient, lax.optimization_barrier(jnp.sum(dzf, axis=1)), lax.optimization_barrier(jnp.sum(dzf, axis=0)), weight_part, gain_partial, bias_part)

def reference(pair_act, pair_cot, pair_mask, pair_norm_gain, pair_norm_bias, proj_weight, left_weight, right_weight):
    block = 2
    count = ROWS // block
    acts = pair_act.reshape(count, block, N, C)
    cots = pair_cot.reshape(count, block, N, C)
    masks = pair_mask.reshape(count, block, N)

    def step(carry, pieces):
        col_acc, weight_acc, gain_acc, bias_acc = carry
        pg, rs, cs, wp, gp, bp = block_terms(pieces[0], pieces[1], pieces[2], pair_norm_gain, pair_norm_bias, proj_weight)
        return ((col_acc + cs, weight_acc + wp, gain_acc + gp, bias_acc + bp), (pg, rs))
    init = (jnp.zeros((N, C), jnp.float32), jnp.zeros((C, C), jnp.float32), jnp.zeros((C,), jnp.float32), jnp.zeros((C,), jnp.float32))
    carry, outs = lax.scan(step, init, (acts, cots, masks))
    col_total, weight_sum, gain_sum, bias_sum = carry
    pair_activation_gradient = outs[0].reshape(ROWS, N, C)
    row_total = outs[1].reshape(ROWS, C)
    scale = 1.0 / jnp.sqrt(jnp.float32(ROWS) * jnp.float32(N))
    row_single_grad = jnp.einsum('rc,sc->rs', row_total, left_weight.astype(jnp.float32), precision=lax.Precision.HIGHEST)
    col_single_grad = jnp.einsum('rc,sc->rs', col_total, right_weight.astype(jnp.float32), precision=lax.Precision.HIGHEST)
    return (pair_activation_gradient, row_single_grad, col_single_grad, weight_sum * scale, gain_sum * scale, bias_sum * scale)
```

```python
import functools

import jax
import jax.numpy as jnp
from jax import lax
from jax.experimental import pallas as pl
from jax.experimental.pallas import tpu as pltpu
from jax.sharding import PartitionSpec as P

EPS = 1e-05
NT = (((1,), (1,)), ((), ()))
COLS = 128
SUB = 32
WIDE = 256
VMEM = 58 << 20


def sums_kernel(x_hbm, cot_hbm, mask_ref, g_ref, send_ref, keep_ref, xv, cv, mf, mv, cc, sems):
    rows, n, c = x_hbm.shape
    chunks = n // COLS
    quarters = COLS // SUB
    bands = rows // quarters
    k = rows * SUB

    def copies(j):
        cols = pl.ds(pl.multiple_of(j * COLS, COLS), COLS)
        return (
            pltpu.make_async_copy(x_hbm.at[:, cols], xv.at[j], sems.at[0, j]),
            pltpu.make_async_copy(cot_hbm.at[:, cols], cv.at[j], sems.at[1, j]),
        )

    for j in range(chunks):
        for copy in copies(j):
            copy.start()
    lane = lax.broadcasted_iota(jnp.int32, (bands, COLS), 1) // SUB
    for j in range(chunks):
        mf[j * rows:(j + 1) * rows, :] = mask_ref[:, j * COLS:(j + 1) * COLS].astype(jnp.float32)
        strips = [mf[pl.ds(j * rows + i, bands, stride=quarters), :] for i in range(quarters)]
        for q in range(quarters):
            mixed = jnp.zeros((bands, COLS), jnp.float32)
            for i in range(quarters):
                shift = ((i - q) * SUB) % COLS
                moved = strips[i] if shift == 0 else pltpu.roll(strips[i], shift, 1)
                mixed = jnp.where(lane == i, moved, mixed)
            mv[q, j, :bands, :] = mixed
    g_ref[...] = jnp.zeros_like(g_ref)
    wide_lane = lax.broadcasted_iota(jnp.int32, (SUB, k), 1)
    wide_sub = lax.broadcasted_iota(jnp.int32, (SUB, k), 0)
    pattern = jnp.concatenate(
        [jnp.where(wide_sub == wide_lane // SUB, 1.0, 0.0), jnp.where(wide_sub == wide_lane % SUB, 1.0, 0.0)], axis=0
    ).astype(jnp.bfloat16)
    r = lax.axis_index("row")
    core = lax.axis_index("col") % 2

    @pl.loop(0, chunks)
    def _(j):
        for copy in copies(j):
            copy.wait()
        total = jnp.zeros((c + SUB, c), jnp.float32)
        columns = []
        for q in range(quarters):
            cot = cv[j, :, q * SUB:(q + 1) * SUB, :].reshape(k, c)
            masks = [mv[q, j, b:b + 1, :] for b in range(bands)]
            parts = []
            for b in range(bands):
                block = xv[j, b * quarters:(b + 1) * quarters, q * SUB:(q + 1) * SUB, :]
                xt = block.reshape(COLS, c).T.astype(jnp.float32)
                xc = xt - jnp.sum(xt, axis=0, keepdims=True) * (1.0 / c)
                var = jnp.sum(xc * xc, axis=0, keepdims=True) * (1.0 / c)
                parts.append((xc * (lax.rsqrt(var + EPS) * masks[b])).astype(jnp.bfloat16))
            mrow = jnp.concatenate([jnp.broadcast_to(m, (16, COLS)).astype(jnp.bfloat16) for m in masks], axis=1)
            lhs = [jnp.concatenate(parts, axis=1)] + [pattern[16 * t:16 * t + 16] * mrow for t in range(4)]
            out = jnp.dot(jnp.concatenate(lhs, axis=0), cot, preferred_element_type=jnp.float32)
            total += out[:c + SUB]
            columns.append(out[c + SUB:])
        for q in range(quarters):
            d = (j * quarters + q) ^ r
            x1, x0, z, y1, y0 = [(d >> s) & 1 for s in (4, 3, 2, 1, 0)]
            px, py = x0 ^ x1, y0 ^ y1
            s4 = jnp.where(core == 0, px, py)
            s3 = jnp.where(core == 0, py, px)
            s2 = jnp.where(core == 0, x1, y1)
            s1 = jnp.where(core == 0, y1, x1)
            off = pl.multiple_of((s4 * 16 + s3 * 8 + s2 * 4 + s1 * 2 + z) * SUB, SUB)
            cc[pl.ds(off, SUB), :] = columns[q]
        g_ref[:c] += total[:c]
        g_ref[c + 8:] += total[c:c + rows]

    keep_ref[...] = cc[:n // 2]
    send_ref[...] = cc[n // 2:]
    g_ref[c:c + 8] = jnp.broadcast_to(jnp.sum(g_ref[c + 8:], axis=0, keepdims=True), (8, c))


def sums(x, cot, mask):
    rows, n, c = x.shape
    vm = pl.BlockSpec(memory_space=pltpu.VMEM)
    hbm = pl.BlockSpec(memory_space=pl.ANY)
    return pl.pallas_call(
        sums_kernel,
        in_specs=[hbm, hbm, vm],
        out_specs=[vm] * 3,
        out_shape=[
            jax.ShapeDtypeStruct((c + 8 + rows, c), jnp.float32),
            jax.ShapeDtypeStruct((n // 2, c), jnp.float32),
            jax.ShapeDtypeStruct((n // 2, c), jnp.float32),
        ],
        scratch_shapes=[
            pltpu.VMEM((n // COLS, rows, COLS, c), jnp.bfloat16),
            pltpu.VMEM((n // COLS, rows, COLS, c), jnp.bfloat16),
            pltpu.VMEM((rows * (n // COLS), COLS), jnp.float32),
            pltpu.VMEM((COLS // SUB, n // COLS, 8, COLS), jnp.float32),
            pltpu.VMEM((n, c), jnp.float32),
            pltpu.SemaphoreType.DMA((2, n // COLS)),
        ],
        compiler_params=pltpu.CompilerParams(vmem_limit_bytes=VMEM),
        name="sums",
    )(x, cot, mask)


def grad_kernel(x_ref, cot_ref, mask_ref, gain_ref, w_ref, out_ref, wt):
    rows, cols, c = x_ref.shape

    @pl.when(pl.program_id(0) == 0)
    def _():
        wg = w_ref[...].astype(jnp.float32) * jnp.broadcast_to(gain_ref[...], (c, c)).T
        wg = wg - jnp.mean(wg, axis=0, keepdims=True)
        high = wg.astype(jnp.bfloat16)
        wt[:c] = high
        wt[c:] = (wg - high.astype(jnp.float32)).astype(jnp.bfloat16)

    p = rows * cols
    both = lax.dot_general(wt[...], cot_ref[...].reshape(p, c), NT, preferred_element_type=jnp.float32)
    dc = both[:c] + both[c:]
    mask = jnp.concatenate([mask_ref[i:i + 1, :].astype(jnp.float32) for i in range(rows)], axis=1)
    xt = x_ref[...].reshape(p, c).T.astype(jnp.float32)
    xc = xt - jnp.sum(xt, axis=0, keepdims=True) * (1.0 / c)
    var = jnp.sum(xc * xc, axis=0, keepdims=True) * (1.0 / c)
    q = jnp.sum(xc * dc, axis=0, keepdims=True) * (1.0 / c)
    rstd = lax.rsqrt(var + EPS)
    masked = rstd * mask
    out = (dc * masked - xc * (masked * rstd * rstd * q)).astype(jnp.bfloat16)
    out_ref[...] = out.T.reshape(rows, cols, c)


def grads(x, cot, mask, gain, w):
    rows, n, c = x.shape
    wide = pl.BlockSpec((rows, WIDE, c), lambda j: (0, j, 0))
    return pl.pallas_call(
        grad_kernel,
        grid=(n // WIDE,),
        in_specs=[
            wide,
            wide,
            pl.BlockSpec((rows, WIDE), lambda j: (0, j)),
            pl.BlockSpec((1, c), lambda j: (0, 0)),
            pl.BlockSpec((c, c), lambda j: (0, 0)),
        ],
        out_specs=wide,
        out_shape=jax.ShapeDtypeStruct((rows, n, c), jnp.bfloat16),
        scratch_shapes=[pltpu.VMEM((2 * c, c), jnp.bfloat16)],
        compiler_params=pltpu.CompilerParams(vmem_limit_bytes=VMEM),
        cost_estimate=pl.CostEstimate(flops=6 * rows * n * c * c, bytes_accessed=6 * rows * n * c, transcendentals=0),
        name="activation_gradient",
    )(x, cot, mask, gain.reshape(1, c), w)


def tail_kernel(g_ref, gain_ref, bias_ref, w_ref, weight_ref, gains_ref, biases_ref, *, scale):
    c = w_ref.shape[0]
    g = g_ref[:c]
    total = g_ref[c:c + 1]
    w = w_ref[...].astype(jnp.float32)
    gain = jnp.broadcast_to(gain_ref[...], (c, c)).T
    bias = jnp.broadcast_to(bias_ref[...], (c, c)).T
    weight_ref[...] = (gain * g + bias * total) * scale
    gains_ref[...] = jnp.sum((w * g).T, axis=0, keepdims=True) * scale
    biases_ref[...] = jnp.sum((w * total).T, axis=0, keepdims=True) * scale


def tail(g, gain, bias, w, scale):
    c = w.shape[0]
    vm = pl.BlockSpec(memory_space=pltpu.VMEM)
    weight, gains, biases = pl.pallas_call(
        functools.partial(tail_kernel, scale=scale),
        in_specs=[vm] * 4,
        out_specs=[vm] * 3,
        out_shape=[
            jax.ShapeDtypeStruct((c, c), jnp.float32),
            jax.ShapeDtypeStruct((1, c), jnp.float32),
            jax.ShapeDtypeStruct((1, c), jnp.float32),
        ],
        name="parameter_gradients",
    )(g, gain.reshape(1, c), bias.reshape(1, c), w)
    return weight, gains.reshape(c), biases.reshape(c)


def flipped(i, move):
    axis, bits = move
    x, z, y, core = i >> 5, ((i >> 4) & 1) * 2 + ((i >> 1) & 1), (i >> 2) & 3, i & 1
    x ^= bits if axis == "x" else 0
    y ^= bits if axis == "y" else 0
    z ^= bits if axis == "z" else 0
    core ^= bits if axis == "core" else 0
    return (((x * 2 + (z >> 1)) * 4 + y) * 2 + (z & 1)) * 2 + core


def exchange(value, move, other=None):
    moves = (move, other or move)
    pairs = [(i, flipped(i, moves[i & 1])) for i in range(128)]
    return lax.ppermute(value, ("row", "col"), pairs)


ORDER = (
    (("x", 1), ("y", 1)),
    (("y", 1), ("x", 1)),
    (("x", 3), ("y", 3)),
    (("y", 3), ("x", 3)),
)


def shards(pair_act, pair_cot, pair_mask, gain, bias, w, left_weight, right_weight):
    rows, n, c = pair_act.shape
    pairs = rows * lax.axis_size("row") * n * lax.axis_size("col")
    scale = 1.0 / float(pairs) ** 0.5
    g, send, keep = sums(pair_act, pair_cot, pair_mask)
    activation_gradient = grads(pair_act, pair_cot, pair_mask, gain, w)

    g = g + exchange(g, ("core", 1))
    g = g + exchange(g, ("z", 1))
    row_total = g[c + 8:]
    g = g[:c + 8]
    size = n // 2
    for move, other in ORDER:
        got = exchange(send, move, other)
        size //= 2
        send = keep[size:] + got[size:]
        keep = keep[:size] + got[:size]
        g = g + exchange(g, move, other)
    g = g + exchange(g, ("z", 3))
    col_total = keep + exchange(send, ("z", 2))

    row_single_grad = jnp.einsum(
        "rc,sc->rs", row_total, left_weight.astype(jnp.float32), precision=lax.Precision.HIGHEST
    )
    col_single_grad = jnp.einsum(
        "rc,sc->rs", col_total, right_weight.astype(jnp.float32), precision=lax.Precision.HIGHEST
    )
    weight_grad, gain_grad, bias_grad = tail(g, gain, bias, w, scale)
    return activation_gradient, row_single_grad, col_single_grad, weight_grad, gain_grad, bias_grad


def solution(mesh):
    in_specs = (
        P("row", "col", None),
        P("row", "col", None),
        P("row", "col"),
        P(),
        P(),
        P(),
        P(),
        P(),
    )
    out_specs = (P("row", "col", None), P("row", None), P(("col", "row"), None), P(), P(), P())
    return jax.shard_map(shards, mesh=mesh, in_specs=in_specs, out_specs=out_specs, check_vma=False)
```

```python
import functools

import jax
import jax.numpy as jnp
from jax import lax
from jax.experimental import pallas as pl
from jax.experimental.pallas import tpu as pltpu
from jax.sharding import PartitionSpec as P

EPS = 1e-05
NT = (((1,), (1,)), ((), ()))
COLS = 128
SUB = 32
VMEM = 38 << 20
SMALL = 4 << 20


def sums_kernel(
    x_hbm, cot_hbm, mask_ref, first_ref, keep_ref, row_ref, xv, cv, mf, mv, cc, sems
):
    rows, n, c = x_hbm.shape
    chunks = n // COLS
    quarters = COLS // SUB
    bands = rows // quarters
    k = rows * SUB

    def copies(j):
        cols = pl.ds(pl.multiple_of(j * COLS, COLS), COLS)
        return (
            pltpu.make_async_copy(x_hbm.at[:, cols], xv.at[j], sems.at[0, j]),
            pltpu.make_async_copy(cot_hbm.at[:, cols], cv.at[j], sems.at[1, j]),
        )

    for j in range(chunks):
        for copy in copies(j):
            copy.start()
    lane = lax.broadcasted_iota(jnp.int32, (bands, COLS), 1) // SUB
    for j in range(chunks):
        mf[j * rows:(j + 1) * rows, :] = mask_ref[:, j * COLS:(j + 1) * COLS].astype(jnp.float32)
        strips = [mf[pl.ds(j * rows + i, bands, stride=quarters), :] for i in range(quarters)]
        for q in range(quarters):
            mixed = jnp.zeros((bands, COLS), jnp.float32)
            for i in range(quarters):
                shift = ((i - q) * SUB) % COLS
                moved = strips[i] if shift == 0 else pltpu.roll(strips[i], shift, 1)
                mixed = jnp.where(lane == i, moved, mixed)
            mv[q, j, :bands, :] = mixed
    first_ref[:c + 8] = jnp.zeros((c + 8, c), jnp.float32)
    row_ref[...] = jnp.zeros_like(row_ref)
    wide_lane = lax.broadcasted_iota(jnp.int32, (SUB, k), 1)
    wide_sub = lax.broadcasted_iota(jnp.int32, (SUB, k), 0)
    pattern = jnp.concatenate(
        [jnp.where(wide_sub == wide_lane // SUB, 1.0, 0.0), jnp.where(wide_sub == wide_lane % SUB, 1.0, 0.0)], axis=0
    ).astype(jnp.bfloat16)
    r = lax.axis_index("row")
    core = lax.axis_index("col") % 2

    @pl.loop(0, chunks)
    def _(j):
        for copy in copies(j):
            copy.wait()
        total = jnp.zeros((c + SUB, c), jnp.float32)
        columns = []
        for q in range(quarters):
            cot = cv[j, :, q * SUB:(q + 1) * SUB, :].reshape(k, c)
            masks = [mv[q, j, b:b + 1, :] for b in range(bands)]
            parts = []
            for b in range(bands):
                block = xv[j, b * quarters:(b + 1) * quarters, q * SUB:(q + 1) * SUB, :]
                xt = block.reshape(COLS, c).T.astype(jnp.float32)
                xc = xt - jnp.sum(xt, axis=0, keepdims=True) * (1.0 / c)
                var = jnp.sum(xc * xc, axis=0, keepdims=True) * (1.0 / c)
                parts.append((xc * (lax.rsqrt(var + EPS) * masks[b])).astype(jnp.bfloat16))
            mrow = jnp.concatenate([jnp.broadcast_to(m, (16, COLS)).astype(jnp.bfloat16) for m in masks], axis=1)
            lhs = [jnp.concatenate(parts, axis=1)] + [pattern[16 * t:16 * t + 16] * mrow for t in range(4)]
            out = jnp.dot(jnp.concatenate(lhs, axis=0), cot, preferred_element_type=jnp.float32)
            total += out[:c + SUB]
            columns.append(out[c + SUB:])
        for q in range(quarters):
            d = (j * quarters + q) ^ r
            x1, x0, z, y1, y0 = [(d >> s) & 1 for s in (4, 3, 2, 1, 0)]
            px, py = x0 ^ x1, y0 ^ y1
            s4 = jnp.where(core == 0, px, py)
            s3 = jnp.where(core == 0, py, px)
            s2 = jnp.where(core == 0, x1, y1)
            s1 = jnp.where(core == 0, y1, x1)
            off = pl.multiple_of((s4 * 16 + s3 * 8 + s2 * 4 + s1 * 2 + z) * SUB, SUB)
            cc[pl.ds(off, SUB), :] = columns[q]
        first_ref[:c] += total[:c]
        row_ref[...] += total[c:c + rows]

    keep_ref[...] = cc[:n // 2]
    first_ref[c + 8:] = cc[n // 2:]
    first_ref[c:c + 8] = jnp.broadcast_to(jnp.sum(row_ref[...], axis=0, keepdims=True), (8, c))


def sums(x, cot, mask):
    rows, n, c = x.shape
    vm = pl.BlockSpec(memory_space=pltpu.VMEM)
    hbm = pl.BlockSpec(memory_space=pl.ANY)
    chunks = jax.ShapeDtypeStruct((n // COLS, rows, COLS, c), jnp.bfloat16)
    return pl.pallas_call(
        sums_kernel,
        in_specs=[hbm, hbm, vm],
        out_specs=[vm] * 5,
        out_shape=[
            jax.ShapeDtypeStruct((c + 8 + n // 2, c), jnp.float32),
            jax.ShapeDtypeStruct((n // 2, c), jnp.float32),
            jax.ShapeDtypeStruct((rows, c), jnp.float32),
            chunks,
            chunks,
        ],
        scratch_shapes=[
            pltpu.VMEM((rows * (n // COLS), COLS), jnp.float32),
            pltpu.VMEM((COLS // SUB, n // COLS, 8, COLS), jnp.float32),
            pltpu.VMEM((n, c), jnp.float32),
            pltpu.SemaphoreType.DMA((2, n // COLS)),
        ],
        compiler_params=pltpu.CompilerParams(vmem_limit_bytes=VMEM),
        name="sums",
    )(x, cot, mask)


def weight_kernel(gain_ref, w_ref, _, wt_ref):
    c = w_ref.shape[0]
    wg = w_ref[...].astype(jnp.float32) * jnp.broadcast_to(gain_ref[...], (c, c)).T
    wg = wg - jnp.mean(wg, axis=0, keepdims=True)
    high = wg.astype(jnp.bfloat16)
    wt_ref[:c] = high
    wt_ref[c:] = (wg - high.astype(jnp.float32)).astype(jnp.bfloat16)


def centred_weight(gain, w, dep):
    c = w.shape[0]
    vm = pl.BlockSpec(memory_space=pltpu.VMEM)
    return pl.pallas_call(
        weight_kernel,
        in_specs=[vm, vm, pl.BlockSpec(memory_space=pl.ANY)],
        out_specs=vm,
        out_shape=jax.ShapeDtypeStruct((2 * c, c), jnp.bfloat16),
        compiler_params=pltpu.CompilerParams(vmem_limit_bytes=SMALL),
        name="centred_weight",
    )(gain.reshape(1, c), w, dep)


def halve_kernel(payload_ref, got_ref, keep_ref, _, next_ref, kept_ref, *, parts):
    size = kept_ref.shape[0]
    next_ref[:parts] = payload_ref[:parts] + got_ref[:parts]
    next_ref[parts:] = keep_ref[size:] + got_ref[parts + size:]
    kept_ref[...] = keep_ref[:size] + got_ref[parts:parts + size]


def halve(payload, got, keep, dep, parts):
    size, c = keep.shape[0] // 2, keep.shape[1]
    vm = pl.BlockSpec(memory_space=pltpu.VMEM)
    return pl.pallas_call(
        functools.partial(halve_kernel, parts=parts),
        in_specs=[vm, vm, vm, pl.BlockSpec(memory_space=pl.ANY)],
        out_specs=[vm, vm],
        out_shape=[jax.ShapeDtypeStruct((parts + size, c), jnp.float32), jax.ShapeDtypeStruct((size, c), jnp.float32)],
        compiler_params=pltpu.CompilerParams(vmem_limit_bytes=SMALL),
        name="halve",
    )(payload, got, keep, dep)


def forward_kernel(payload_ref, got_ref, _, next_ref, row_ref, *, parts):
    rows = row_ref.shape[0]
    next_ref[:parts] = payload_ref[:parts] + got_ref[:parts]
    row_ref[...] = payload_ref[parts:parts + rows] + got_ref[parts:parts + rows]
    next_ref[parts:] = got_ref[parts + rows:]


def forward(payload, got, dep, parts, rows):
    size, c = payload.shape[0] - parts - rows, payload.shape[1]
    vm = pl.BlockSpec(memory_space=pltpu.VMEM)
    return pl.pallas_call(
        functools.partial(forward_kernel, parts=parts),
        in_specs=[vm, vm, pl.BlockSpec(memory_space=pl.ANY)],
        out_specs=[vm, vm],
        out_shape=[jax.ShapeDtypeStruct((parts + size, c), jnp.float32), jax.ShapeDtypeStruct((rows, c), jnp.float32)],
        compiler_params=pltpu.CompilerParams(vmem_limit_bytes=SMALL),
        name="forward",
    )(payload, got, dep)


def piece_kernel(*refs, first, count, before, last):
    refs = list(refs)
    xv, cv, mask_ref, wt_ref, _ = refs[:5]
    refs = refs[5:]
    prev = refs.pop(0) if before else None
    if before and first - before > 0:
        refs.pop(0)
    now = refs.pop(0)
    out = refs.pop(0) if before else None
    sems = refs.pop(0)
    rows, c = xv.shape[1], xv.shape[3]
    p = rows * COLS

    def away(buffer, t, j):
        return pltpu.make_async_copy(buffer.at[t], out.at[:, pl.ds(j * COLS, COLS)], sems.at[j])

    copies = [away(prev, t, first - before + t) for t in range(before)]
    for copy in copies:
        copy.start()
    for t in range(count):
        j = first + t
        both = lax.dot_general(wt_ref[...], cv[j].reshape(p, c), NT, preferred_element_type=jnp.float32)
        dc = both[:c] + both[c:]
        mask = jnp.concatenate(
            [mask_ref[i:i + 1, j * COLS:(j + 1) * COLS].astype(jnp.float32) for i in range(rows)], axis=1
        )
        xt = xv[j].reshape(p, c).T.astype(jnp.float32)
        xc = xt - jnp.sum(xt, axis=0, keepdims=True) * (1.0 / c)
        var = jnp.sum(xc * xc, axis=0, keepdims=True) * (1.0 / c)
        q = jnp.sum(xc * dc, axis=0, keepdims=True) * (1.0 / c)
        rstd = lax.rsqrt(var + EPS)
        masked = rstd * mask
        grad = (dc * masked - xc * (masked * rstd * rstd * q)).astype(jnp.bfloat16)
        now[t] = grad.T.reshape(rows, COLS, c)
        if last:
            copies.append(away(now, t, j))
            copies[-1].start()
    for copy in copies:
        copy.wait()


def piece(xv, cv, mask, wt, dep, prev, out, *, first, count):
    chunks, rows, cols, c = xv.shape
    n = chunks * cols
    vm = pl.BlockSpec(memory_space=pltpu.VMEM)
    hbm = pl.BlockSpec(memory_space=pl.ANY)
    before = 0 if prev is None else prev.shape[0]
    operands = [xv, cv, mask, wt, dep]
    in_specs = [vm] * 4 + [hbm]
    aliases = {}
    out_specs = [vm]
    out_shape = [jax.ShapeDtypeStruct((count, rows, cols, c), jnp.bfloat16)]
    if before:
        operands.append(prev)
        in_specs.append(vm)
        if out is not None:
            operands.append(out)
            in_specs.append(hbm)
            aliases = {6: 1}
        out_specs.append(hbm)
        out_shape.append(jax.ShapeDtypeStruct((rows, n, c), jnp.bfloat16))
    pairs = count * rows * cols
    results = pl.pallas_call(
        functools.partial(piece_kernel, first=first, count=count, before=before, last=first + count == chunks),
        in_specs=in_specs,
        out_specs=out_specs,
        out_shape=out_shape,
        scratch_shapes=[pltpu.SemaphoreType.DMA((chunks,))],
        input_output_aliases=aliases,
        compiler_params=pltpu.CompilerParams(vmem_limit_bytes=VMEM),
        cost_estimate=pl.CostEstimate(flops=6 * pairs * c * c, bytes_accessed=6 * pairs * c, transcendentals=0),
        name="gradient_piece",
    )(*operands)
    return results[0], (results[1] if before else None)


def tail_kernel(g_ref, got_ref, keep_ref, gain_ref, bias_ref, w_ref, right_ref, weight_ref, gains_ref, biases_ref, col_ref, *, scale):
    c = w_ref.shape[0]
    g = g_ref[:c] + got_ref[:c]
    total = g_ref[c:c + 1] + got_ref[c:c + 1]
    w = w_ref[...].astype(jnp.float32)
    gain = jnp.broadcast_to(gain_ref[...], (c, c)).T
    bias = jnp.broadcast_to(bias_ref[...], (c, c)).T
    weight_ref[...] = (gain * g + bias * total) * scale
    gains_ref[...] = jnp.sum((w * g).T, axis=0, keepdims=True) * scale
    biases_ref[...] = jnp.sum((w * total).T, axis=0, keepdims=True) * scale
    col_total = keep_ref[...] + got_ref[c + 8:]
    col_ref[...] = lax.dot_general(
        col_total, right_ref[...].astype(jnp.float32), NT,
        precision=lax.Precision.HIGHEST, preferred_element_type=jnp.float32,
    )


def tail(g, got, keep, gain, bias, w, right, scale):
    c = w.shape[0]
    vm = pl.BlockSpec(memory_space=pltpu.VMEM)
    weight, gains, biases, col = pl.pallas_call(
        functools.partial(tail_kernel, scale=scale),
        in_specs=[vm] * 7,
        out_specs=[vm] * 4,
        out_shape=[
            jax.ShapeDtypeStruct((c, c), jnp.float32),
            jax.ShapeDtypeStruct((1, c), jnp.float32),
            jax.ShapeDtypeStruct((1, c), jnp.float32),
            jax.ShapeDtypeStruct((keep.shape[0], right.shape[0]), jnp.float32),
        ],
        compiler_params=pltpu.CompilerParams(vmem_limit_bytes=SMALL),
        name="parameter_gradients",
    )(g, got, keep, gain.reshape(1, c), bias.reshape(1, c), w, right)
    return weight, gains.reshape(c), biases.reshape(c), col


def flipped(i, move):
    axis, bits = move
    x, z, y, core = i >> 5, ((i >> 4) & 1) * 2 + ((i >> 1) & 1), (i >> 2) & 3, i & 1
    x ^= bits if axis == "x" else 0
    y ^= bits if axis == "y" else 0
    z ^= bits if axis == "z" else 0
    core ^= bits if axis == "core" else 0
    return (((x * 2 + (z >> 1)) * 4 + y) * 2 + (z & 1)) * 2 + core


def exchange(value, move, other=None):
    moves = (move, other or move)
    pairs = [(i, flipped(i, moves[i & 1])) for i in range(128)]
    return lax.ppermute(value, ("row", "col"), pairs)


ORDER = (
    (("x", 1), ("y", 1)),
    (("y", 1), ("x", 1)),
    (("x", 3), ("y", 3)),
    (("y", 3), ("x", 3)),
)


PIECES = ((0, 2), (2, 2), (4, 1), (5, 1), (6, 1), (7, 1))


def shards(pair_act, pair_cot, pair_mask, gain, bias, w, left_weight, right_weight):
    rows, n, c = pair_act.shape
    pairs = rows * lax.axis_size("row") * n * lax.axis_size("col")
    scale = 1.0 / float(pairs) ** 0.5
    parts = c + 8
    payload, keep, row_part, xv, cv = sums(pair_act, pair_cot, pair_mask)
    wt = centred_weight(gain, w, payload)
    prev = out = None
    pieces = list(PIECES)

    def work(dep):
        first, count = pieces.pop(0)
        return piece(xv, cv, pair_mask, wt, dep, prev, out, first=first, count=count)

    for move, other in ORDER:
        got = exchange(payload, move, other)
        prev, out = work(payload)
        payload, keep = halve(payload, got, keep, prev, parts)
    send = payload[parts:]
    payload = jnp.concatenate([payload[:parts], row_part], axis=0)
    payload = payload + exchange(payload, ("core", 1))
    payload = jnp.concatenate([payload, send], axis=0)
    got = exchange(payload, ("z", 1))
    prev, out = work(payload)
    payload, row_total = forward(payload, got, prev, parts, rows)
    got = exchange(payload, ("z", 3))
    prev, out = work(payload)

    row_single_grad = jnp.einsum(
        "rc,sc->rs", row_total, left_weight.astype(jnp.float32), precision=lax.Precision.HIGHEST
    )
    weight_grad, gain_grad, bias_grad, col_single_grad = tail(payload, got, keep, gain, bias, w, right_weight, scale)
    return out, row_single_grad, col_single_grad, weight_grad, gain_grad, bias_grad


def solution(mesh):
    in_specs = (
        P("row", "col", None),
        P("row", "col", None),
        P("row", "col"),
        P(),
        P(),
        P(),
        P(),
        P(),
    )
    out_specs = (P("row", "col", None), P("row", None), P(("col", "row"), None), P(), P(), P())
    return jax.shard_map(shards, mesh=mesh, in_specs=in_specs, out_specs=out_specs, check_vma=False)
```

```python
import functools

import jax
import jax.numpy as jnp
from jax import lax
from jax.experimental import pallas as pl
from jax.experimental.pallas import tpu as pltpu
from jax.sharding import PartitionSpec as P

EPS = 1e-05
NT = (((1,), (1,)), ((), ()))
COLS = 128
SUB = 32
HOLD = 38 << 20
PIECE = 16 << 20
SMALL = 4 << 20


def sums_kernel(
    x_hbm, cot_hbm, mask_hbm, g_ref, send_ref, keep_ref, xv, cv, mask_ref, mf, mv, cc, sems, mask_sem
):
    rows, n, c = x_hbm.shape
    chunks = n // COLS
    quarters = COLS // SUB
    bands = rows // quarters
    k = rows * SUB

    def copies(j):
        cols = pl.ds(pl.multiple_of(j * COLS, COLS), COLS)
        return (
            pltpu.make_async_copy(x_hbm.at[:, cols], xv.at[j], sems.at[0, j]),
            pltpu.make_async_copy(cot_hbm.at[:, cols], cv.at[j], sems.at[1, j]),
        )

    mask_copy = pltpu.make_async_copy(mask_hbm, mask_ref, mask_sem)
    mask_copy.start()
    for j in range(chunks):
        for copy in copies(j):
            copy.start()
    mask_copy.wait()
    lane = lax.broadcasted_iota(jnp.int32, (bands, COLS), 1) // SUB
    for j in range(chunks):
        mf[j * rows:(j + 1) * rows, :] = mask_ref[:, j * COLS:(j + 1) * COLS].astype(jnp.float32)
        strips = [mf[pl.ds(j * rows + i, bands, stride=quarters), :] for i in range(quarters)]
        for q in range(quarters):
            mixed = jnp.zeros((bands, COLS), jnp.float32)
            for i in range(quarters):
                shift = ((i - q) * SUB) % COLS
                moved = strips[i] if shift == 0 else pltpu.roll(strips[i], shift, 1)
                mixed = jnp.where(lane == i, moved, mixed)
            mv[q, j, :bands, :] = mixed
    g_ref[...] = jnp.zeros_like(g_ref)
    wide_lane = lax.broadcasted_iota(jnp.int32, (SUB, k), 1)
    wide_sub = lax.broadcasted_iota(jnp.int32, (SUB, k), 0)
    pattern = jnp.concatenate(
        [jnp.where(wide_sub == wide_lane // SUB, 1.0, 0.0), jnp.where(wide_sub == wide_lane % SUB, 1.0, 0.0)], axis=0
    ).astype(jnp.bfloat16)
    r = lax.axis_index("row")
    core = lax.axis_index("col") % 2

    @pl.loop(0, chunks)
    def _(j):
        for copy in copies(j):
            copy.wait()
        total = jnp.zeros((c + SUB, c), jnp.float32)
        columns = []
        for q in range(quarters):
            cot = cv[j, :, q * SUB:(q + 1) * SUB, :].reshape(k, c)
            masks = [mv[q, j, b:b + 1, :] for b in range(bands)]
            parts = []
            for b in range(bands):
                block = xv[j, b * quarters:(b + 1) * quarters, q * SUB:(q + 1) * SUB, :]
                xt = block.reshape(COLS, c).T.astype(jnp.float32)
                xc = xt - jnp.sum(xt, axis=0, keepdims=True) * (1.0 / c)
                var = jnp.sum(xc * xc, axis=0, keepdims=True) * (1.0 / c)
                parts.append((xc * (lax.rsqrt(var + EPS) * masks[b])).astype(jnp.bfloat16))
            mrow = jnp.concatenate([jnp.broadcast_to(m, (16, COLS)).astype(jnp.bfloat16) for m in masks], axis=1)
            lhs = [jnp.concatenate(parts, axis=1)] + [pattern[16 * t:16 * t + 16] * mrow for t in range(4)]
            out = jnp.dot(jnp.concatenate(lhs, axis=0), cot, preferred_element_type=jnp.float32)
            total += out[:c + SUB]
            columns.append(out[c + SUB:])
        for q in range(quarters):
            d = (j * quarters + q) ^ r
            x1, x0, z, y1, y0 = [(d >> s) & 1 for s in (4, 3, 2, 1, 0)]
            px, py = x0 ^ x1, y0 ^ y1
            s4 = jnp.where(core == 0, px, py)
            s3 = jnp.where(core == 0, py, px)
            s2 = jnp.where(core == 0, x1, y1)
            s1 = jnp.where(core == 0, y1, x1)
            off = pl.multiple_of((s4 * 16 + s3 * 8 + s2 * 4 + s1 * 2 + z) * SUB, SUB)
            cc[pl.ds(off, SUB), :] = columns[q]
        g_ref[:c] += total[:c]
        g_ref[c + 8:] += total[c:c + rows]

    keep_ref[...] = cc[:n // 2]
    send_ref[...] = cc[n // 2:]
    g_ref[c:c + 8] = jnp.broadcast_to(jnp.sum(g_ref[c + 8:], axis=0, keepdims=True), (8, c))


def sums(x, cot, mask):
    rows, n, c = x.shape
    vm = pl.BlockSpec(memory_space=pltpu.VMEM)
    hbm = pl.BlockSpec(memory_space=pl.ANY)
    chunks = jax.ShapeDtypeStruct((n // COLS, rows, COLS, c), jnp.bfloat16)
    return pl.pallas_call(
        sums_kernel,
        in_specs=[hbm, hbm, hbm],
        out_specs=[vm] * 5,
        out_shape=[
            jax.ShapeDtypeStruct((c + 8 + rows, c), jnp.float32),
            jax.ShapeDtypeStruct((n // 2, c), jnp.float32),
            jax.ShapeDtypeStruct((n // 2, c), jnp.float32),
            chunks,
            chunks,
        ],
        scratch_shapes=[
            pltpu.VMEM((rows, n), jnp.int32),
            pltpu.VMEM((rows * (n // COLS), COLS), jnp.float32),
            pltpu.VMEM((COLS // SUB, n // COLS, 8, COLS), jnp.float32),
            pltpu.VMEM((n, c), jnp.float32),
            pltpu.SemaphoreType.DMA((2, n // COLS)),
            pltpu.SemaphoreType.DMA,
        ],
        compiler_params=pltpu.CompilerParams(vmem_limit_bytes=HOLD),
        name="sums",
    )(x, cot, mask)


def weight_kernel(gain_ref, w_ref, _, wt_ref):
    c = w_ref.shape[0]
    wg = w_ref[...].astype(jnp.float32) * jnp.broadcast_to(gain_ref[...], (c, c)).T
    wg = wg - jnp.mean(wg, axis=0, keepdims=True)
    high = wg.astype(jnp.bfloat16)
    wt_ref[:c] = high
    wt_ref[c:] = (wg - high.astype(jnp.float32)).astype(jnp.bfloat16)


def centred_weight(gain, w, dep):
    c = w.shape[0]
    vm = pl.BlockSpec(memory_space=pltpu.VMEM)
    return pl.pallas_call(
        weight_kernel,
        in_specs=[vm, vm, pl.BlockSpec(memory_space=pl.ANY)],
        out_specs=vm,
        out_shape=jax.ShapeDtypeStruct((2 * c, c), jnp.bfloat16),
        compiler_params=pltpu.CompilerParams(vmem_limit_bytes=SMALL),
        name="centred_weight",
    )(gain.reshape(1, c), w, dep)


def halve_kernel(payload_ref, got_ref, col_ref, keep_ref, _, next_ref, kept_ref, *, parts):
    size = kept_ref.shape[0]
    at = col_ref.shape[0] - 2 * size
    next_ref[:parts] = payload_ref[:parts] + got_ref[:parts]
    next_ref[parts:] = keep_ref[size:] + col_ref[at + size:]
    kept_ref[...] = keep_ref[:size] + col_ref[at:at + size]


def halve(payload, got, col, keep, dep, parts):
    size, c = keep.shape[0] // 2, keep.shape[1]
    vm = pl.BlockSpec(memory_space=pltpu.VMEM)
    return pl.pallas_call(
        functools.partial(halve_kernel, parts=parts),
        in_specs=[vm, vm, vm, vm, pl.BlockSpec(memory_space=pl.ANY)],
        out_specs=[vm, vm],
        out_shape=[jax.ShapeDtypeStruct((parts + size, c), jnp.float32), jax.ShapeDtypeStruct((size, c), jnp.float32)],
        compiler_params=pltpu.CompilerParams(vmem_limit_bytes=SMALL),
        name="halve",
    )(payload, got, col, keep, dep)


def forward_kernel(payload_ref, got_ref, _, next_ref, row_ref, *, parts):
    rows = row_ref.shape[0]
    next_ref[:parts] = payload_ref[:parts] + got_ref[:parts]
    row_ref[...] = payload_ref[parts:parts + rows] + got_ref[parts:parts + rows]
    next_ref[parts:] = got_ref[parts + rows:]


def forward(payload, got, dep, parts, rows):
    size, c = payload.shape[0] - parts - rows, payload.shape[1]
    vm = pl.BlockSpec(memory_space=pltpu.VMEM)
    return pl.pallas_call(
        functools.partial(forward_kernel, parts=parts),
        in_specs=[vm, vm, pl.BlockSpec(memory_space=pl.ANY)],
        out_specs=[vm, vm],
        out_shape=[jax.ShapeDtypeStruct((parts + size, c), jnp.float32), jax.ShapeDtypeStruct((rows, c), jnp.float32)],
        compiler_params=pltpu.CompilerParams(vmem_limit_bytes=SMALL),
        name="forward",
    )(payload, got, dep)


def piece_kernel(*refs, first, count, before, last):
    refs = list(refs)
    xv, cv, mask_ref, wt_ref, _ = refs[:5]
    refs = refs[5:]
    prev = refs.pop(0) if before else None
    if before and first - before > 0:
        refs.pop(0)
    now = refs.pop(0)
    out = refs.pop(0) if before else None
    sems = refs.pop(0)
    rows, c = xv.shape[1], xv.shape[3]
    p = rows * COLS

    def away(buffer, t, j):
        return pltpu.make_async_copy(buffer.at[t], out.at[:, pl.ds(j * COLS, COLS)], sems.at[j])

    copies = [away(prev, t, first - before + t) for t in range(before)]
    for copy in copies:
        copy.start()
    for t in range(count):
        j = first + t
        both = lax.dot_general(wt_ref[...], cv[j].reshape(p, c), NT, preferred_element_type=jnp.float32)
        dc = both[:c] + both[c:]
        mask = jnp.concatenate(
            [mask_ref[i:i + 1, j * COLS:(j + 1) * COLS].astype(jnp.float32) for i in range(rows)], axis=1
        )
        xt = xv[j].reshape(p, c).T.astype(jnp.float32)
        xc = xt - jnp.sum(xt, axis=0, keepdims=True) * (1.0 / c)
        var = jnp.sum(xc * xc, axis=0, keepdims=True) * (1.0 / c)
        q = jnp.sum(xc * dc, axis=0, keepdims=True) * (1.0 / c)
        rstd = lax.rsqrt(var + EPS)
        masked = rstd * mask
        grad = (dc * masked - xc * (masked * rstd * rstd * q)).astype(jnp.bfloat16)
        now[t] = grad.T.reshape(rows, COLS, c)
        if last:
            copies.append(away(now, t, j))
            copies[-1].start()
    for copy in copies:
        copy.wait()


def piece(xv, cv, mask, wt, dep, prev, out, *, first, count):
    chunks, rows, cols, c = xv.shape
    n = chunks * cols
    vm = pl.BlockSpec(memory_space=pltpu.VMEM)
    hbm = pl.BlockSpec(memory_space=pl.ANY)
    before = 0 if prev is None else prev.shape[0]
    operands = [xv, cv, mask, wt, dep]
    in_specs = [vm] * 4 + [hbm]
    aliases = {}
    out_specs = [vm]
    out_shape = [jax.ShapeDtypeStruct((count, rows, cols, c), jnp.bfloat16)]
    if before:
        operands.append(prev)
        in_specs.append(vm)
        if out is not None:
            operands.append(out)
            in_specs.append(hbm)
            aliases = {6: 1}
        out_specs.append(hbm)
        out_shape.append(jax.ShapeDtypeStruct((rows, n, c), jnp.bfloat16))
    pairs = count * rows * cols
    results = pl.pallas_call(
        functools.partial(piece_kernel, first=first, count=count, before=before, last=first + count == chunks),
        in_specs=in_specs,
        out_specs=out_specs,
        out_shape=out_shape,
        scratch_shapes=[pltpu.SemaphoreType.DMA((chunks,))],
        input_output_aliases=aliases,
        compiler_params=pltpu.CompilerParams(vmem_limit_bytes=PIECE),
        cost_estimate=pl.CostEstimate(flops=6 * pairs * c * c, bytes_accessed=6 * pairs * c, transcendentals=0),
        name="gradient_piece",
    )(*operands)
    return results[0], (results[1] if before else None)


def tail_kernel(g_ref, got_ref, keep_ref, gain_ref, bias_ref, w_ref, right_ref, weight_ref, gains_ref, biases_ref, col_ref, *, scale):
    c = w_ref.shape[0]
    g = g_ref[:c] + got_ref[:c]
    total = g_ref[c:c + 1] + got_ref[c:c + 1]
    w = w_ref[...].astype(jnp.float32)
    gain = jnp.broadcast_to(gain_ref[...], (c, c)).T
    bias = jnp.broadcast_to(bias_ref[...], (c, c)).T
    weight_ref[...] = (gain * g + bias * total) * scale
    gains_ref[...] = jnp.sum((w * g).T, axis=0, keepdims=True) * scale
    biases_ref[...] = jnp.sum((w * total).T, axis=0, keepdims=True) * scale
    col_total = keep_ref[...] + got_ref[c + 8:]
    col_ref[...] = lax.dot_general(
        col_total, right_ref[...].astype(jnp.float32), NT,
        precision=lax.Precision.HIGHEST, preferred_element_type=jnp.float32,
    )


def tail(g, got, keep, gain, bias, w, right, scale):
    c = w.shape[0]
    vm = pl.BlockSpec(memory_space=pltpu.VMEM)
    weight, gains, biases, col = pl.pallas_call(
        functools.partial(tail_kernel, scale=scale),
        in_specs=[vm] * 7,
        out_specs=[vm] * 4,
        out_shape=[
            jax.ShapeDtypeStruct((c, c), jnp.float32),
            jax.ShapeDtypeStruct((1, c), jnp.float32),
            jax.ShapeDtypeStruct((1, c), jnp.float32),
            jax.ShapeDtypeStruct((keep.shape[0], right.shape[0]), jnp.float32),
        ],
        compiler_params=pltpu.CompilerParams(vmem_limit_bytes=SMALL),
        name="parameter_gradients",
    )(g, got, keep, gain.reshape(1, c), bias.reshape(1, c), w, right)
    return weight, gains.reshape(c), biases.reshape(c), col


def flipped(i, move):
    axis, bits = move
    x, z, y, core = i >> 5, ((i >> 4) & 1) * 2 + ((i >> 1) & 1), (i >> 2) & 3, i & 1
    x ^= bits if axis == "x" else 0
    y ^= bits if axis == "y" else 0
    z ^= bits if axis == "z" else 0
    core ^= bits if axis == "core" else 0
    return (((x * 2 + (z >> 1)) * 4 + y) * 2 + (z & 1)) * 2 + core


def exchange(value, move, other=None):
    moves = (move, other or move)
    pairs = [(i, flipped(i, moves[i & 1])) for i in range(128)]
    return lax.ppermute(value, ("row", "col"), pairs)


ORDER = (
    (("x", 1), ("y", 1)),
    (("y", 1), ("x", 1)),
    (("x", 3), ("y", 3)),
    (("y", 3), ("x", 3)),
)


PIECES = ((0, 3), (3, 2), (5, 2), (7, 1))


def shards(pair_act, pair_cot, pair_mask, gain, bias, w, left_weight, right_weight):
    rows, n, c = pair_act.shape
    pairs = rows * lax.axis_size("row") * n * lax.axis_size("col")
    scale = 1.0 / float(pairs) ** 0.5
    parts = c + 8
    sums_here, send, keep, xv, cv = sums(pair_act, pair_cot, pair_mask)
    wt = centred_weight(gain, w, sums_here)
    prev = out = None
    col = exchange(send, *ORDER[0])
    sums_here = sums_here + exchange(sums_here, ("core", 1))
    payload, row_part = sums_here[:parts], sums_here[parts:]
    for step, (move, other) in enumerate(ORDER):
        got = exchange(payload, move, other)
        first, count = PIECES[step]
        prev, out = piece(xv, cv, pair_mask, wt, payload, prev, out, first=first, count=count)
        payload, keep = halve(payload, got, got if step else col, keep, prev, parts)
    payload = jnp.concatenate([payload[:parts], row_part, payload[parts:]], axis=0)
    got = exchange(payload, ("z", 1))
    payload, row_total = forward(payload, got, prev, parts, rows)
    got = exchange(payload, ("z", 3))

    row_single_grad = jnp.einsum(
        "rc,sc->rs", row_total, left_weight.astype(jnp.float32), precision=lax.Precision.HIGHEST
    )
    weight_grad, gain_grad, bias_grad, col_single_grad = tail(payload, got, keep, gain, bias, w, right_weight, scale)
    return out, row_single_grad, col_single_grad, weight_grad, gain_grad, bias_grad


def solution(mesh):
    in_specs = (
        P("row", "col", None),
        P("row", "col", None),
        P("row", "col"),
        P(),
        P(),
        P(),
        P(),
        P(),
    )
    out_specs = (P("row", "col", None), P("row", None), P(("col", "row"), None), P(), P(), P())
    return jax.shard_map(shards, mesh=mesh, in_specs=in_specs, out_specs=out_specs, check_vma=False)
```

```python
import functools

import jax
import jax.numpy as jnp
from jax import lax
from jax.experimental import pallas as pl
from jax.experimental.pallas import tpu as pltpu
from jax.sharding import PartitionSpec as P

EPS = 1e-05
NT = (((1,), (1,)), ((), ()))
COLS = 128
SUB = 32
HOLD = 38 << 20
PIECE = 16 << 20
SMALL = 4 << 20


def sums_kernel(
    x_hbm, cot_hbm, mask_hbm, g_ref, send_ref, keep_ref, xv, cv, mf, mask_ref, mv, cc, sems, mask_sem
):
    rows, n, c = x_hbm.shape
    chunks = n // COLS
    quarters = COLS // SUB
    bands = rows // quarters
    k = rows * SUB

    def copies(j):
        cols = pl.ds(pl.multiple_of(j * COLS, COLS), COLS)
        return (
            pltpu.make_async_copy(x_hbm.at[:, cols], xv.at[j], sems.at[0, j]),
            pltpu.make_async_copy(cot_hbm.at[:, cols], cv.at[j], sems.at[1, j]),
        )

    mask_copy = pltpu.make_async_copy(mask_hbm, mask_ref, mask_sem)
    mask_copy.start()
    for j in range(1):
        for copy in copies(j):
            copy.start()
    mask_copy.wait()
    for j in range(1, chunks):
        for copy in copies(j):
            copy.start()
    lane = lax.broadcasted_iota(jnp.int32, (bands, COLS), 1) // SUB
    for j in range(chunks):
        mf[j * rows:(j + 1) * rows, :] = mask_ref[:, j * COLS:(j + 1) * COLS].astype(jnp.float32)
        strips = [mf[pl.ds(j * rows + i, bands, stride=quarters), :] for i in range(quarters)]
        for q in range(quarters):
            mixed = jnp.zeros((bands, COLS), jnp.float32)
            for i in range(quarters):
                shift = ((i - q) * SUB) % COLS
                moved = strips[i] if shift == 0 else pltpu.roll(strips[i], shift, 1)
                mixed = jnp.where(lane == i, moved, mixed)
            mv[q, j, :bands, :] = mixed
    g_ref[...] = jnp.zeros_like(g_ref)
    wide_lane = lax.broadcasted_iota(jnp.int32, (SUB, k), 1)
    wide_sub = lax.broadcasted_iota(jnp.int32, (SUB, k), 0)
    pattern = jnp.concatenate(
        [jnp.where(wide_sub == wide_lane // SUB, 1.0, 0.0), jnp.where(wide_sub == wide_lane % SUB, 1.0, 0.0)], axis=0
    ).astype(jnp.bfloat16)
    r = lax.axis_index("row")
    core = lax.axis_index("col") % 2

    @pl.loop(0, chunks)
    def _(j):
        for copy in copies(j):
            copy.wait()
        total = jnp.zeros((c + SUB, c), jnp.float32)
        columns = []
        for q in range(quarters):
            cot = cv[j, :, q * SUB:(q + 1) * SUB, :].reshape(k, c)
            masks = [mv[q, j, b:b + 1, :] for b in range(bands)]
            parts = []
            for b in range(bands):
                block = xv[j, b * quarters:(b + 1) * quarters, q * SUB:(q + 1) * SUB, :]
                xt = block.reshape(COLS, c).T.astype(jnp.float32)
                xc = xt - jnp.sum(xt, axis=0, keepdims=True) * (1.0 / c)
                var = jnp.sum(xc * xc, axis=0, keepdims=True) * (1.0 / c)
                parts.append((xc * (lax.rsqrt(var + EPS) * masks[b])).astype(jnp.bfloat16))
            mrow = jnp.concatenate([jnp.broadcast_to(m, (16, COLS)).astype(jnp.bfloat16) for m in masks], axis=1)
            lhs = [jnp.concatenate(parts, axis=1)] + [pattern[16 * t:16 * t + 16] * mrow for t in range(4)]
            out = jnp.dot(jnp.concatenate(lhs, axis=0), cot, preferred_element_type=jnp.float32)
            total += out[:c + SUB]
            columns.append(out[c + SUB:])
        for q in range(quarters):
            d = (j * quarters + q) ^ r
            x1, x0, z, y1, y0 = [(d >> s) & 1 for s in (4, 3, 2, 1, 0)]
            px, py = x0 ^ x1, y0 ^ y1
            s4 = jnp.where(core == 0, px, py)
            s3 = jnp.where(core == 0, py, px)
            s2 = jnp.where(core == 0, x1, y1)
            s1 = jnp.where(core == 0, y1, x1)
            off = pl.multiple_of((s4 * 16 + s3 * 8 + s2 * 4 + s1 * 2 + z) * SUB, SUB)
            cc[pl.ds(off, SUB), :] = columns[q]
        g_ref[:c] += total[:c]
        g_ref[c + 8:] += total[c:c + rows]

    keep_ref[...] = cc[:n // 2]
    send_ref[...] = cc[n // 2:]
    g_ref[c:c + 8] = jnp.broadcast_to(jnp.sum(g_ref[c + 8:], axis=0, keepdims=True), (8, c))


def sums(x, cot, mask):
    rows, n, c = x.shape
    vm = pl.BlockSpec(memory_space=pltpu.VMEM)
    hbm = pl.BlockSpec(memory_space=pl.ANY)
    chunks = jax.ShapeDtypeStruct((n // COLS, rows, COLS, c), jnp.bfloat16)
    return pl.pallas_call(
        sums_kernel,
        in_specs=[hbm, hbm, hbm],
        out_specs=[vm] * 6,
        out_shape=[
            jax.ShapeDtypeStruct((c + 8 + rows, c), jnp.float32),
            jax.ShapeDtypeStruct((n // 2, c), jnp.float32),
            jax.ShapeDtypeStruct((n // 2, c), jnp.float32),
            chunks,
            chunks,
            jax.ShapeDtypeStruct((rows * (n // COLS), COLS), jnp.float32),
        ],
        scratch_shapes=[
            pltpu.VMEM((rows, n), jnp.int32),
            pltpu.VMEM((COLS // SUB, n // COLS, 8, COLS), jnp.float32),
            pltpu.VMEM((n, c), jnp.float32),
            pltpu.SemaphoreType.DMA((2, n // COLS)),
            pltpu.SemaphoreType.DMA,
        ],
        compiler_params=pltpu.CompilerParams(vmem_limit_bytes=HOLD),
        name="sums",
    )(x, cot, mask)


def weight_kernel(gain_ref, w_ref, _, wt_ref):
    c = w_ref.shape[0]
    wg = w_ref[...].astype(jnp.float32) * jnp.broadcast_to(gain_ref[...], (c, c)).T
    wg = wg - jnp.mean(wg, axis=0, keepdims=True)
    high = wg.astype(jnp.bfloat16)
    wt_ref[:c] = high
    wt_ref[c:] = (wg - high.astype(jnp.float32)).astype(jnp.bfloat16)


def centred_weight(gain, w, dep):
    c = w.shape[0]
    vm = pl.BlockSpec(memory_space=pltpu.VMEM)
    return pl.pallas_call(
        weight_kernel,
        in_specs=[vm, vm, pl.BlockSpec(memory_space=pl.ANY)],
        out_specs=vm,
        out_shape=jax.ShapeDtypeStruct((2 * c, c), jnp.bfloat16),
        compiler_params=pltpu.CompilerParams(vmem_limit_bytes=SMALL),
        name="centred_weight",
    )(gain.reshape(1, c), w, dep)


def halve_kernel(payload_ref, got_ref, col_ref, keep_ref, _, next_ref, kept_ref, *, parts):
    size = kept_ref.shape[0]
    at = col_ref.shape[0] - 2 * size
    next_ref[:parts] = payload_ref[:parts] + got_ref[:parts]
    next_ref[parts:] = keep_ref[size:] + col_ref[at + size:]
    kept_ref[...] = keep_ref[:size] + col_ref[at:at + size]


def halve(payload, got, col, keep, dep, parts):
    size, c = keep.shape[0] // 2, keep.shape[1]
    vm = pl.BlockSpec(memory_space=pltpu.VMEM)
    return pl.pallas_call(
        functools.partial(halve_kernel, parts=parts),
        in_specs=[vm, vm, vm, vm, pl.BlockSpec(memory_space=pl.ANY)],
        out_specs=[vm, vm],
        out_shape=[jax.ShapeDtypeStruct((parts + size, c), jnp.float32), jax.ShapeDtypeStruct((size, c), jnp.float32)],
        compiler_params=pltpu.CompilerParams(vmem_limit_bytes=SMALL),
        name="halve",
    )(payload, got, col, keep, dep)


def forward_kernel(payload_ref, got_ref, _, next_ref, row_ref, *, parts):
    rows = row_ref.shape[0]
    next_ref[:parts] = payload_ref[:parts] + got_ref[:parts]
    row_ref[...] = payload_ref[parts:parts + rows] + got_ref[parts:parts + rows]
    next_ref[parts:] = got_ref[parts + rows:]


def forward(payload, got, dep, parts, rows):
    size, c = payload.shape[0] - parts - rows, payload.shape[1]
    vm = pl.BlockSpec(memory_space=pltpu.VMEM)
    return pl.pallas_call(
        functools.partial(forward_kernel, parts=parts),
        in_specs=[vm, vm, pl.BlockSpec(memory_space=pl.ANY)],
        out_specs=[vm, vm],
        out_shape=[jax.ShapeDtypeStruct((parts + size, c), jnp.float32), jax.ShapeDtypeStruct((rows, c), jnp.float32)],
        compiler_params=pltpu.CompilerParams(vmem_limit_bytes=SMALL),
        name="forward",
    )(payload, got, dep)


def piece_kernel(*refs, first, count, before, last):
    refs = list(refs)
    xv, cv, mask_ref, wt_ref, _ = refs[:5]
    refs = refs[5:]
    prev = refs.pop(0) if before else None
    if before and first - before > 0:
        refs.pop(0)
    now = refs.pop(0)
    out = refs.pop(0) if before else None
    sems = refs.pop(0)
    rows, c = xv.shape[1], xv.shape[3]
    p = rows * COLS

    def away(buffer, t, j):
        return pltpu.make_async_copy(buffer.at[t], out.at[:, pl.ds(j * COLS, COLS)], sems.at[j])

    copies = [away(prev, t, first - before + t) for t in range(before)]
    for copy in copies:
        copy.start()
    for t in range(count):
        j = first + t
        both = lax.dot_general(wt_ref[...], cv[j].reshape(p, c), NT, preferred_element_type=jnp.float32)
        dc = both[:c] + both[c:]
        mask = jnp.concatenate(
            [mask_ref[j * rows + i:j * rows + i + 1, :] for i in range(rows)], axis=1
        )
        xt = xv[j].reshape(p, c).T.astype(jnp.float32)
        xc = xt - jnp.sum(xt, axis=0, keepdims=True) * (1.0 / c)
        var = jnp.sum(xc * xc, axis=0, keepdims=True) * (1.0 / c)
        q = jnp.sum(xc * dc, axis=0, keepdims=True) * (1.0 / c)
        rstd = lax.rsqrt(var + EPS)
        masked = rstd * mask
        grad = (dc * masked - xc * (masked * rstd * rstd * q)).astype(jnp.bfloat16)
        now[t] = grad.T.reshape(rows, COLS, c)
        if last:
            copies.append(away(now, t, j))
            copies[-1].start()
    for copy in copies:
        copy.wait()


def piece(xv, cv, mask, wt, dep, prev, out, *, first, count):
    chunks, rows, cols, c = xv.shape
    n = chunks * cols
    vm = pl.BlockSpec(memory_space=pltpu.VMEM)
    hbm = pl.BlockSpec(memory_space=pl.ANY)
    before = 0 if prev is None else prev.shape[0]
    operands = [xv, cv, mask, wt, dep]
    in_specs = [vm] * 4 + [hbm]
    aliases = {}
    out_specs = [vm]
    out_shape = [jax.ShapeDtypeStruct((count, rows, cols, c), jnp.bfloat16)]
    if before:
        operands.append(prev)
        in_specs.append(vm)
        if out is not None:
            operands.append(out)
            in_specs.append(hbm)
            aliases = {6: 1}
        out_specs.append(hbm)
        out_shape.append(jax.ShapeDtypeStruct((rows, n, c), jnp.bfloat16))
    pairs = count * rows * cols
    results = pl.pallas_call(
        functools.partial(piece_kernel, first=first, count=count, before=before, last=first + count == chunks),
        in_specs=in_specs,
        out_specs=out_specs,
        out_shape=out_shape,
        scratch_shapes=[pltpu.SemaphoreType.DMA((chunks,))],
        input_output_aliases=aliases,
        compiler_params=pltpu.CompilerParams(vmem_limit_bytes=PIECE),
        cost_estimate=pl.CostEstimate(flops=6 * pairs * c * c, bytes_accessed=6 * pairs * c, transcendentals=0),
        name="gradient_piece",
    )(*operands)
    return results[0], (results[1] if before else None)


def tail_kernel(g_ref, got_ref, keep_ref, gain_ref, bias_ref, w_ref, right_ref, weight_ref, gains_ref, biases_ref, col_ref, *, scale):
    c = w_ref.shape[0]
    g = g_ref[:c] + got_ref[:c]
    total = g_ref[c:c + 1] + got_ref[c:c + 1]
    w = w_ref[...].astype(jnp.float32)
    gain = jnp.broadcast_to(gain_ref[...], (c, c)).T
    bias = jnp.broadcast_to(bias_ref[...], (c, c)).T
    weight_ref[...] = (gain * g + bias * total) * scale
    gains_ref[...] = jnp.sum((w * g).T, axis=0, keepdims=True) * scale
    biases_ref[...] = jnp.sum((w * total).T, axis=0, keepdims=True) * scale
    col_total = keep_ref[...] + got_ref[c + 8:]
    col_ref[...] = lax.dot_general(
        col_total, right_ref[...].astype(jnp.float32), NT,
        precision=lax.Precision.HIGHEST, preferred_element_type=jnp.float32,
    )


def tail(g, got, keep, gain, bias, w, right, scale):
    c = w.shape[0]
    vm = pl.BlockSpec(memory_space=pltpu.VMEM)
    weight, gains, biases, col = pl.pallas_call(
        functools.partial(tail_kernel, scale=scale),
        in_specs=[vm] * 7,
        out_specs=[vm] * 4,
        out_shape=[
            jax.ShapeDtypeStruct((c, c), jnp.float32),
            jax.ShapeDtypeStruct((1, c), jnp.float32),
            jax.ShapeDtypeStruct((1, c), jnp.float32),
            jax.ShapeDtypeStruct((keep.shape[0], right.shape[0]), jnp.float32),
        ],
        compiler_params=pltpu.CompilerParams(vmem_limit_bytes=SMALL),
        name="parameter_gradients",
    )(g, got, keep, gain.reshape(1, c), bias.reshape(1, c), w, right)
    return weight, gains.reshape(c), biases.reshape(c), col


def flipped(i, move):
    axis, bits = move
    x, z, y, core = i >> 5, ((i >> 4) & 1) * 2 + ((i >> 1) & 1), (i >> 2) & 3, i & 1
    x ^= bits if axis == "x" else 0
    y ^= bits if axis == "y" else 0
    z ^= bits if axis == "z" else 0
    core ^= bits if axis == "core" else 0
    return (((x * 2 + (z >> 1)) * 4 + y) * 2 + (z & 1)) * 2 + core


def exchange(value, move, other=None):
    moves = (move, other or move)
    pairs = [(i, flipped(i, moves[i & 1])) for i in range(128)]
    return lax.ppermute(value, ("row", "col"), pairs)


ORDER = (
    (("x", 1), ("y", 1)),
    (("y", 1), ("x", 1)),
    (("x", 3), ("y", 3)),
    (("y", 3), ("x", 3)),
)


PIECES = ((0, 3), (3, 2), (5, 2), (7, 1))


def shards(pair_act, pair_cot, pair_mask, gain, bias, w, left_weight, right_weight):
    rows, n, c = pair_act.shape
    pairs = rows * lax.axis_size("row") * n * lax.axis_size("col")
    scale = 1.0 / float(pairs) ** 0.5
    parts = c + 8
    sums_here, send, keep, xv, cv, masks = sums(pair_act, pair_cot, pltpu.with_memory_space_constraint(pair_mask, pltpu.HBM))
    wt = centred_weight(gain, w, sums_here)
    prev = out = None
    col = exchange(send, *ORDER[0])
    sums_here = sums_here + exchange(sums_here, ("core", 1))
    payload, row_part = sums_here[:parts], sums_here[parts:]
    for step, (move, other) in enumerate(ORDER):
        got = exchange(payload, move, other)
        first, count = PIECES[step]
        prev, out = piece(xv, cv, masks, wt, payload, prev, out, first=first, count=count)
        payload, keep = halve(payload, got, got if step else col, keep, prev, parts)
    payload = jnp.concatenate([payload[:parts], row_part, payload[parts:]], axis=0)
    got = exchange(payload, ("z", 1))
    payload, row_total = forward(payload, got, prev, parts, rows)
    got = exchange(payload, ("z", 3))

    row_single_grad = jnp.einsum(
        "rc,sc->rs", row_total, left_weight.astype(jnp.float32), precision=lax.Precision.HIGHEST
    )
    weight_grad, gain_grad, bias_grad, col_single_grad = tail(payload, got, keep, gain, bias, w, right_weight, scale)
    return out, row_single_grad, col_single_grad, weight_grad, gain_grad, bias_grad


def solution(mesh):
    in_specs = (
        P("row", "col", None),
        P("row", "col", None),
        P("row", "col"),
        P(),
        P(),
        P(),
        P(),
        P(),
    )
    out_specs = (P("row", "col", None), P("row", None), P(("col", "row"), None), P(), P(), P())
    return jax.shard_map(shards, mesh=mesh, in_specs=in_specs, out_specs=out_specs, check_vma=False)
```
